512 devices in a mesh: dp: 32 (over y, x, core), tensor: 16 (over z).
Axes of the slice: x: 4, y: 4, z: 16, core: 2. Of those that a mesh axis runs over, the one named last changes fastest.
Arguments:
- attention: bfloat16 [16384, 5120], P(('dp', 'tensor')), may hold values from -6 to 6
- residual: bfloat16 [16384, 5120], P('dp', 'tensor'), may hold values from -6 to 6
- output_weight: bfloat16 [5120, 5120], P(None, 'tensor'), may hold values from -0.078125 to 0.078125
- adapter_down_weight: bfloat16 [256, 5120, 64], P('dp', 'tensor'), may hold values from -0.078125 to 0.078125
- adapter_up_weight: bfloat16 [256, 64, 5120], P('dp', None, 'tensor'), may hold values from -0.75 to 0.75
- tenant: int32 [4096], P('dp'), may hold values from 0 to 255, as said below
- adapter_slot_index: int32 [256], replicated, may hold values from 0 to 255, as said below
Outputs:
- hidden: bfloat16 [16384, 5120], P('dp', 'tensor')
The draws below stay inside these ranges and needn't reach their ends.
Inputs may be any that keep to these rules, and one draw needn't show every extreme that they name: With owner = adapter_slot_index[tenant] // 8: one index of dp, the same for all, is the owner of exactly 12 of the requests of every index of dp; every other index of dp owns at most 4 of the requests of one index of dp, and exactly 4 for some. A permutation: adapter a is row adapter_slot_index[a] of adapter_down_weight and adapter_up_weight.
All inputs are finite; a program needn't handle non-finite values.
Results may differ from the reference program's by a relative error of at most 0.0028.
Values may be sent and summed in bfloat16 or wider, within the bound.
A program may use at most 64 MiB of HBM per device.

```python
import jax
import jax.numpy as jnp
from jax import lax

MODEL_WIDTH = 5120
ADAPTER_RANK = 64
DRAFT = 4
ADP_DEV = 8
REQ_DEV = 128
TOKENS = 16384
TENANT_ADAPTERS = 256
CAP = 12


def shared_draw(key):
    slot_order = jax.random.permutation(jax.random.fold_in(key, 11), TENANT_ADAPTERS).astype(jnp.int32)
    owner_count = TENANT_ADAPTERS // ADP_DEV
    hot_owner = jax.random.randint(jax.random.fold_in(key, 12), (), 0, owner_count)
    return (slot_order, hot_owner)


def draw_adapter_slot_index(key, part):
    slot_order, hot_owner = shared_draw(key)
    return slot_order


def draw_tenant(key, part):
    slot_order, hot_owner = shared_draw(key)
    key = jax.random.fold_in(key, 5)
    owner_count = TENANT_ADAPTERS // ADP_DEV
    key_shift, key_order, key_local = jax.random.split(key, 3)
    shifts = jax.random.randint(key_shift, (owner_count, 1), 0, owner_count - 1)
    positions = jnp.arange(REQ_DEV, dtype=jnp.int32)[None, :]
    spread_owner = (hot_owner + 1 + (positions - CAP + shifts) % (owner_count - 1)) % owner_count
    owners = jnp.where(positions < CAP, hot_owner, spread_owner)
    order_keys = jax.random.split(key_order, owner_count)
    orders = jax.vmap(lambda single: jax.random.permutation(single, REQ_DEV))(order_keys)
    owners = jnp.take_along_axis(owners, orders, axis=1)
    local_ids = jax.random.randint(key_local, (owner_count, REQ_DEV), 0, ADP_DEV)
    inverse = jnp.argsort(slot_order).astype(jnp.int32)
    tenants = inverse[owners * ADP_DEV + local_ids]
    return tenants.reshape(owner_count * REQ_DEV).astype(jnp.int32)


def block_scale(key, shape, cuts, low, top_value):
    def one(axis_at, shards_of):
        steps = jax.random.uniform(jax.random.fold_in(jax.random.fold_in(key, 6), axis_at), (shards_of,), jnp.float32, low / len(cuts), top_value / len(cuts))
        return jnp.repeat(jnp.exp(steps), shape[axis_at] // shards_of).reshape((-1,) + (1,) * (len(shape) - axis_at - 1))

    loudness = one(*cuts[0])
    for cut in cuts[1:]:
        loudness = loudness * one(*cut)
    return loudness


def normal_values(own_key, extent, width, reach, shards=(), held_as=jnp.bfloat16):
    values = jax.random.normal(own_key, extent, jnp.float32) * width
    if len(shards) > 0:
        values = block_scale(own_key, extent, shards, -0.22, 0.18) * values
    return jnp.clip(values, min=-reach, max=reach).astype(held_as)


def setup_inputs(seed: int = 0) -> dict:
    seeds = jax.random.split(jax.random.key(seed), 8)
    return {
        "attention": normal_values(seeds[0], (TOKENS, MODEL_WIDTH), 1.0, 6.0, ((0, 512),)),
        "residual": normal_values(seeds[1], (TOKENS, MODEL_WIDTH), 1.0, 6.0, ((0, 32), (1, 16))),
        "output_weight": normal_values(seeds[2], (MODEL_WIDTH, MODEL_WIDTH), MODEL_WIDTH ** -0.5, 0.078125, ((1, 16),)),
        "adapter_down_weight": normal_values(seeds[3], (TENANT_ADAPTERS, MODEL_WIDTH, ADAPTER_RANK), MODEL_WIDTH ** -0.5, 0.078125, ((0, 32), (1, 16))),
        "adapter_up_weight": normal_values(seeds[4], (TENANT_ADAPTERS, ADAPTER_RANK, MODEL_WIDTH), ADAPTER_RANK ** -0.5, 0.75, ((0, 32), (2, 16))),
        "tenant": draw_tenant(jax.random.fold_in(seeds[7], 71), 0),
        "adapter_slot_index": draw_adapter_slot_index(jax.random.fold_in(seeds[7], 71), 0),
    }


adapter_scale = 0.5


def reference(attention, residual, output_weight, adapter_down_weight, adapter_up_weight, tenant, adapter_slot_index):
    base_output = jnp.dot(attention, output_weight, preferred_element_type=jnp.float32)
    request_slots = adapter_slot_index[tenant].astype(jnp.int32)
    row_blocks = attention.reshape(-1, REQ_DEV, DRAFT, MODEL_WIDTH)
    slot_blocks = request_slots.reshape(-1, REQ_DEV)

    def one_block(block_args):
        block_row_group, block_slot_group = block_args
        down_weight_maps = adapter_down_weight[block_slot_group].astype(jnp.float32)
        shrink_step = jnp.einsum("mzi,mix->mzx", block_row_group.astype(jnp.float32), down_weight_maps).astype(jnp.bfloat16)
        shrink_step = lax.optimization_barrier(shrink_step)
        up_weight_maps = adapter_up_weight[block_slot_group].astype(jnp.float32)
        return jnp.einsum("uav,uvh->uah", shrink_step.astype(jnp.float32), up_weight_maps).astype(jnp.bfloat16)

    expand_step = lax.map(one_block, (row_blocks, slot_blocks)).reshape(TOKENS, MODEL_WIDTH)
    expand_step = lax.optimization_barrier(expand_step)
    total_output = residual.astype(jnp.float32) + base_output + adapter_scale * expand_step.astype(jnp.float32)
    return total_output.astype(jnp.bfloat16)
```

```python
import jax
import jax.numpy as jnp
from jax import lax
from jax.experimental import pallas as pl
from jax.experimental.pallas import tpu as pltpu
from jax.sharding import PartitionSpec as P

BF = jnp.bfloat16
F32 = jnp.float32
ND, NZ = 32, 16
DRAFT, REQ, TOK = 4, 128, 512
WIDTH, COLS, RANK, ADP = 5120, 320, 64, 8
OWN = TOK // NZ
SLOT = TOK // ND
AROWS = 1536
ACH = AROWS // ND
BCH = ADP * RANK // ND
KCH = 512


def iota(shape, axis):
    return lax.broadcasted_iota(jnp.int32, shape, axis)


def dot(a, b):
    return jnp.dot(a, b, preferred_element_type=F32)


def dot_t(a, b):
    return lax.dot_general(a, b, (((0,), (0,)), ((), ())), preferred_element_type=F32)


def onehot(mask):
    return jnp.where(mask, 1.0, 0.0).astype(BF)


def routing(tenant, index, me):
    hit = onehot(iota((2 * REQ, REQ), 0) == tenant)
    slot = dot(jnp.broadcast_to(index, (8, 2 * REQ)).astype(F32).astype(BF), hit)[0:1]
    owner = jnp.floor(slot * (1.0 / ADP))
    adapter = slot - ADP * owner
    owner_id = iota((ND, REQ), 0).astype(F32)
    own_hit = jnp.where(owner_id == owner, 1.0, 0.0)
    before = onehot(iota((REQ, REQ), 0) < iota((REQ, REQ), 1))
    place = jnp.sum(own_hit * dot(own_hit.astype(BF), before), axis=0, keepdims=True)
    count = jnp.sum(own_hit, axis=1, keepdims=True)
    busy = jnp.where(count > 4.5, 1.0, 0.0)
    busy_req = jnp.sum(own_hit * busy, axis=0, keepdims=True)
    count = jnp.broadcast_to(count * (1.0 - busy), (ND, REQ)).astype(BF)
    is_busy = jnp.sum(busy * jnp.where(owner_id[:, 0:1] == me.astype(F32), 1.0, 0.0), axis=0, keepdims=True)
    slot_row = iota((REQ, REQ), 0)
    filled = dot(onehot(iota((REQ, ND), 0) // 4 == iota((REQ, ND), 1)), count)
    free = jnp.where((slot_row % 4).astype(F32) >= filled, 1.0, 0.0)
    rank = dot(onehot(iota((REQ, REQ), 1) < slot_row), free.astype(BF))
    to_free = free * jnp.where(rank == place, 1.0, 0.0) * busy_req
    to_own = jnp.where(slot_row.astype(F32) == 4.0 * owner + place, 1.0, 0.0) * (1.0 - busy_req)
    by_request = (to_free + to_own).astype(BF)
    spread = onehot(iota((REQ, TOK), 0) == iota((REQ, TOK), 1) // DRAFT)
    gather = onehot(iota((TOK, REQ), 0) // DRAFT == iota((TOK, REQ), 1))
    rows = dot(dot(gather, by_request).astype(BF), spread)
    same = iota((TOK, TOK), 0) % DRAFT == iota((TOK, TOK), 1) % DRAFT
    matrix = jnp.where(same, rows, 0.0).astype(BF)
    ident = adapter + 1.0 + ADP * busy_req
    eye = iota((REQ, REQ), 0) == iota((REQ, REQ), 1)
    column = jnp.sum(jnp.where(eye, ident, 0.0), axis=1, keepdims=True)
    ids = dot(gather, jnp.broadcast_to(column, (REQ, 64)).astype(BF)).astype(BF)
    return matrix, ids, is_busy


def kernel(att, res_h, w_h, a_h, b_h, ten, idx, out, w, res, av, bv, apk, asnd, bsnd, arcv, brcv, ahot, bhot,
           snd, own, pick, pk, prcv, zs, zr, red, sh, er, back, buf, base,
           lsem, sa, ra, sg, rg, shs, shr, sha, sra, sd, rd, sz, rz, sy, ry, sb, rb):
    d = lax.axis_index("dp")
    z = lax.axis_index("tensor")

    def copy(src, dst, ss, rs, dev):
        return pltpu.make_async_remote_copy(src_ref=src, dst_ref=dst, send_sem=ss, recv_sem=rs, device_id=dev,
                                            device_id_type=pl.DeviceIdType.MESH)

    def zdev(i):
        return (d, lax.rem(z + i, NZ))

    def ddev(i):
        return (lax.rem(d + i, ND), z)

    def each(n, f):
        def body(i, carry):
            f(i)
            return carry
        lax.fori_loop(1, n, body, 0)

    barrier = pltpu.get_barrier_semaphore()
    each(NZ, lambda i: pl.semaphore_signal(barrier, inc=1, device_id=zdev(i), device_id_type=pl.DeviceIdType.MESH))
    each(ND, lambda i: pl.semaphore_signal(barrier, inc=1, device_id=ddev(i), device_id_type=pl.DeviceIdType.MESH))
    loads = [pltpu.make_async_copy(h, v, lsem.at[i]) for i, (h, v) in
             enumerate(((a_h, av), (b_h, bv), (w_h, w), (res_h, res)))]
    for load in loads:
        load.start()
    for t in range(NZ):
        snd[t] = att[:, COLS * t:COLS * t + COLS]
    matrix, ids, is_busy = routing(ten[...], idx[...], d)
    pick[...] = matrix
    own[z] = snd[z]
    loads[0].wait()
    loads[1].wait()
    mine = is_busy.astype(BF)
    for e in range(4):
        pair = jnp.concatenate([av[e], av[e + 4]], axis=1)
        apk[COLS * e:COLS * e + COLS] = pair
        asnd[COLS * e:COLS * e + COLS] = pair * mine
    asnd[4 * COLS:] = jnp.zeros((AROWS - 4 * COLS, 128), BF)
    for e in range(ADP):
        bsnd[RANK * e:RANK * e + RANK] = bv[e] * mine
    arcv[d] = asnd[pl.ds(pl.multiple_of(d * ACH, 16), ACH)]
    brcv[d] = bsnd[pl.ds(pl.multiple_of(d * BCH, 16), BCH)]
    pl.semaphore_wait(barrier, NZ + ND - 2)

    def slices(i):
        to = lax.rem(z + i, NZ)
        return copy(snd.at[to], own.at[z], sa.at[i], ra.at[i], (d, to))

    each(NZ, lambda i: slices(i).start())

    right, left = zdev(1), zdev(NZ - 1)

    def ring(way, step, half):
        block = lax.rem(z + (NZ - step if way == 0 else step), NZ)
        dst = buf.at[block, pl.ds(16 * half, 16)]
        src = att.at[pl.ds(16 * half, 16)] if step == 0 else dst
        return copy(src, dst, sg.at[way, step, half], rg.at[way, step, half], right if way == 0 else left)

    def moves(step):
        return [(way, half) for half in range(2) for way in range(2) if step < 7 or way == half]

    def ring_step(step):
        for way, half in moves(step):
            if step > 0:
                ring(way, step - 1, half).wait_recv()
            ring(way, step, half).start()

    ring_step(0)

    def scatter(i):
        to = lax.rem(d + i, ND)
        return (copy(asnd.at[pl.ds(pl.multiple_of(to * ACH, 16), ACH)], arcv.at[d], shs.at[i], shr.at[i], (to, z)),
                copy(bsnd.at[pl.ds(pl.multiple_of(to * BCH, 16), BCH)], brcv.at[d], sha.at[i], sra.at[i], (to, z)))

    def spread_hot(i):
        return (copy(ahot.at[d], ahot.at[d], shs.at[ND + i], shr.at[ND + i], ddev(i)),
                copy(bhot.at[d], bhot.at[d], sha.at[ND + i], sra.at[ND + i], ddev(i)))

    def start_both(pair):
        pair[0].start()
        pair[1].start()

    def wait_both(pair):
        pair[0].wait_recv()
        pair[1].wait_recv()

    def sent_both(pair):
        pair[0].wait_send()
        pair[1].wait_send()

    each(ND, lambda i: start_both(scatter(i)))
    buf[z] = att[...]
    each(ND, lambda i: wait_both(scatter(i)))
    ahot[d] = jnp.sum(arcv[...].astype(F32), axis=0).astype(BF)
    bhot[d] = jnp.sum(brcv[...].astype(F32), axis=0).astype(BF)
    each(ND, lambda i: start_both(spread_hot(i)))

    each(NZ, lambda i: slices(i).wait_recv())
    ext = jnp.concatenate([own[...].reshape(TOK, COLS), ids], axis=1)
    pk[...] = dot(pick[...], ext).astype(BF).reshape(ND, SLOT, COLS + 64)
    prcv[d] = pk[d]

    def deliver(i):
        to = lax.rem(d + i, ND)
        return copy(pk.at[to], prcv.at[d], sd.at[i], rd.at[i], (to, z))

    each(ND, lambda i: deliver(i).start())
    ring_step(1)
    each(ND, lambda i: wait_both(spread_hot(i)))
    each(ND, lambda i: deliver(i).wait_recv())
    got = prcv[...].reshape(TOK, COLS + 64)
    rows, ident = got[:, :COLS], got[:, COLS:COLS + 1].astype(F32)
    upper = jnp.where(iota((1, 128), 1) < RANK, 0.0, 4.0)
    hot_a = ahot[...].reshape(AROWS, 128)
    total = jnp.zeros((TOK, 128), F32)
    for e in range(4):
        lane_id = upper + (e + 1.0)
        total += jnp.where(ident == lane_id, dot(rows, apk[COLS * e:COLS * e + COLS]), 0.0)
        total += jnp.where(ident == lane_id + ADP, dot(rows, hot_a[COLS * e:COLS * e + COLS]), 0.0)
    part = (total[:, :RANK] + total[:, RANK:]).astype(BF)
    for t in range(NZ):
        zs[t] = jnp.concatenate([part[32 * t:32 * t + 16], part[32 * t + 16:32 * t + 32]], axis=1)
    zr[z] = zs[z]

    def reduce(i):
        to = lax.rem(z + i, NZ)
        return copy(zs.at[to], zr.at[z], sz.at[i], rz.at[i], (d, to))

    def share(i):
        return copy(red.at[z], red.at[z], sy.at[i], ry.at[i], zdev(i))

    each(NZ, lambda i: reduce(i).start())
    ring_step(2)
    each(NZ, lambda i: reduce(i).wait_recv())
    red[z] = jnp.sum(zr[...].astype(F32), axis=0).astype(BF)
    each(NZ, lambda i: share(i).start())
    ring_step(3)
    each(NZ, lambda i: share(i).wait_recv())
    for t in range(NZ):
        sh[32 * t:32 * t + 16] = red[t, :, :RANK]
        sh[32 * t + 16:32 * t + 32] = red[t, :, RANK:]
    wide = jnp.concatenate([sh[...]] * ADP, axis=1)
    group = (iota((1, ADP * RANK), 1) // RANK + 1).astype(F32)
    zero = jnp.zeros((), BF)
    expand = dot(jnp.where(ident == group, wide, zero), bv[...].reshape(ADP * RANK, COLS))
    expand += dot(jnp.where(ident == group + ADP, wide, zero), bhot[...].reshape(ADP * RANK, COLS))
    er[...] = expand.astype(BF).reshape(ND, SLOT, COLS)
    back[d] = er[d]

    def give_back(i):
        to = lax.rem(d + i, ND)
        return copy(er.at[to], back.at[d], sb.at[i], rb.at[i], (to, z))

    each(ND, lambda i: give_back(i).start())
    ring_step(4)
    loads[2].wait()
    loads[3].wait()

    def project(steps):
        blocks = [lax.rem(z + s + NZ, NZ) for s in steps]

        def body(k, acc):
            at = pl.ds(pl.multiple_of(k * KCH, KCH), KCH)
            x = jnp.concatenate([buf[b, :, at] for b in blocks], axis=0)
            return acc + dot(x, w[at, :])

        acc = lax.fori_loop(0, WIDTH // KCH, body, jnp.zeros((OWN * len(blocks), COLS), F32))
        for n, b in enumerate(blocks):
            base[pl.ds(pl.multiple_of(b * OWN, OWN), OWN)] = acc[OWN * n:OWN * n + OWN]

    project([0, -1, 1, -2, 2, -3, 3, -4, 4])
    ring_step(5)
    each(ND, lambda i: give_back(i).wait_recv())
    extra = dot_t(pick[...], back[...].reshape(TOK, COLS))
    ring_step(6)
    project([-5, 5, -6, 6])
    ring_step(7)
    for way, half in moves(6):
        if (way, half) not in moves(7):
            ring(way, 6, half).wait_recv()
    for way, half in moves(7):
        ring(way, 7, half).wait_recv()
    project([-7, 7, 8])
    out[...] = (res[...].astype(F32) + base[...] + 0.5 * extra).astype(BF)

    for step in range(8):
        for way, half in moves(step):
            ring(way, step, half).wait_send()
    each(NZ, lambda i: slices(i).wait_send())
    each(NZ, lambda i: reduce(i).wait_send())
    each(NZ, lambda i: share(i).wait_send())
    each(ND, lambda i: sent_both(scatter(i)))
    each(ND, lambda i: sent_both(spread_hot(i)))
    each(ND, lambda i: deliver(i).wait_send())
    each(ND, lambda i: give_back(i).wait_send())


def local(attention, residual, output_weight, adapter_down_weight, adapter_up_weight, tenant, adapter_slot_index):
    vmem = pl.BlockSpec(memory_space=pltpu.VMEM)
    hbm = pl.BlockSpec(memory_space=pl.ANY)
    dma = pltpu.SemaphoreType.DMA

    def held(*shape, dtype=BF):
        return pltpu.VMEM(shape, dtype)

    return pl.pallas_call(
        kernel,
        out_shape=jax.ShapeDtypeStruct((TOK, COLS), BF),
        in_specs=[vmem, hbm, hbm, hbm, hbm, vmem, vmem],
        out_specs=vmem,
        scratch_shapes=[
            held(WIDTH, COLS), held(TOK, COLS), held(ADP, COLS, RANK), held(ADP, RANK, COLS),
            held(4 * COLS, 128), held(AROWS, 128), held(ADP * RANK, COLS),
            held(ND, ACH, 128), held(ND, BCH, COLS), held(ND, ACH, 128), held(ND, BCH, COLS),
            held(NZ, OWN, COLS), held(NZ, OWN, COLS), held(TOK, TOK),
            held(ND, SLOT, COLS + 64), held(ND, SLOT, COLS + 64),
            held(NZ, 16, 128), held(NZ, 16, 128), held(NZ, 16, 128), held(TOK, RANK),
            held(ND, SLOT, COLS), held(ND, SLOT, COLS),
            held(NZ, OWN, WIDTH), held(TOK, COLS, dtype=F32),
            dma((4,)), dma((NZ,)), dma((NZ,)), dma((2, 8, 2)), dma((2, 8, 2)),
            dma((2 * ND,)), dma((2 * ND,)), dma((2 * ND,)), dma((2 * ND,)),
            dma((ND,)), dma((ND,)), dma((NZ,)), dma((NZ,)), dma((NZ,)), dma((NZ,)), dma((ND,)), dma((ND,)),
        ],
        compiler_params=pltpu.CompilerParams(collective_id=0, has_side_effects=True, vmem_limit_bytes=56 * 2**20),
    )(attention, residual, output_weight, adapter_down_weight, adapter_up_weight,
      tenant.reshape(1, REQ), adapter_slot_index.reshape(1, 2 * REQ))


def solution(mesh):
    in_specs = (
        P(("dp", "tensor"), None),
        P("dp", "tensor"),
        P(None, "tensor"),
        P("dp", "tensor", None),
        P("dp", None, "tensor"),
        P("dp"),
        P(),
    )
    return jax.shard_map(local, mesh=mesh, in_specs=in_specs, out_specs=P("dp", "tensor"), check_vma=False)
```

```python
import jax
import jax.numpy as jnp
from jax import lax
from jax.experimental import pallas as pl
from jax.experimental.pallas import tpu as pltpu
from jax.sharding import PartitionSpec as P

BF = jnp.bfloat16
F32 = jnp.float32
ND, NZ = 32, 16
DRAFT, REQ, TOK = 4, 128, 512
WIDTH, COLS, RANK, ADP = 5120, 320, 64, 8
OWN = TOK // NZ
SLOT = TOK // ND
HOT = ADP * RANK
HALF = WIDTH // 2
NC = 16
MAIN, REST = 256, 64
QUART = HALF // 4
LANES = HALF + QUART
CUT = 1664


def iota(shape, axis):
    return lax.broadcasted_iota(jnp.int32, shape, axis)


def dot(a, b):
    return jnp.dot(a, b, preferred_element_type=F32)


def dot_t(a, b):
    return lax.dot_general(a, b, (((0,), (0,)), ((), ())), preferred_element_type=F32)


def onehot(mask):
    return jnp.where(mask, 1.0, 0.0).astype(BF)


def dot_nt(a, b):
    return lax.dot_general(a, b, (((1,), (1,)), ((), ())), preferred_element_type=F32)


def routing(tenant, index, me):
    hit = onehot(iota((2 * REQ, REQ), 0) == tenant)
    slot = dot(jnp.broadcast_to(index, (8, 2 * REQ)).astype(F32).astype(BF), hit)[0:1]
    owner = jnp.floor(slot * (1.0 / ADP))
    adapter = slot - ADP * owner
    owner_id = iota((ND, REQ), 0).astype(F32)
    own_hit = jnp.where(owner_id == owner, 1.0, 0.0)
    before = onehot(iota((REQ, REQ), 0) < iota((REQ, REQ), 1))
    place = jnp.sum(own_hit * dot(own_hit.astype(BF), before), axis=0, keepdims=True)
    count = jnp.sum(own_hit, axis=1, keepdims=True)
    busy = jnp.where(count > 4.5, 1.0, 0.0)
    busy_req = jnp.sum(own_hit * busy, axis=0, keepdims=True)
    count = jnp.broadcast_to(count * (1.0 - busy), (ND, REQ)).astype(BF)
    is_busy = jnp.sum(busy * jnp.where(owner_id[:, 0:1] == me.astype(F32), 1.0, 0.0), axis=0, keepdims=True)
    slot_row = iota((REQ, REQ), 0)
    filled = dot(onehot(iota((REQ, ND), 0) // 4 == iota((REQ, ND), 1)), count)
    free = jnp.where((slot_row % 4).astype(F32) >= filled, 1.0, 0.0)
    rank = dot(onehot(iota((REQ, REQ), 1) < slot_row), free.astype(BF))
    to_free = free * jnp.where(rank == place, 1.0, 0.0) * busy_req
    to_own = jnp.where(slot_row.astype(F32) == 4.0 * owner + place, 1.0, 0.0) * (1.0 - busy_req)
    by_request = (to_free + to_own).astype(BF)
    spread = onehot(iota((REQ, TOK), 0) == iota((REQ, TOK), 1) // DRAFT)
    gather = onehot(iota((TOK, REQ), 0) // DRAFT == iota((TOK, REQ), 1))
    rows = dot(dot(gather, by_request).astype(BF), spread)
    same = iota((TOK, TOK), 0) % DRAFT == iota((TOK, TOK), 1) % DRAFT
    matrix = jnp.where(same, rows, 0.0).astype(BF)
    ident = adapter + 1.0 + ADP * busy_req
    eye = iota((REQ, REQ), 0) == iota((REQ, REQ), 1)
    column = jnp.sum(jnp.where(eye, ident, 0.0), axis=1, keepdims=True)
    ids = dot(gather, jnp.broadcast_to(column, (REQ, 64)).astype(BF)).astype(BF)
    return matrix, ids, is_busy


def kernel(att, res_h, w_h, a_h, b_h, ten, idx, out, wr, res, av, bv, mine, twin_in, half, hot_in, hot,
           snd, own, pick, pk, prcv, zs, zr, red, sh, er, back, buf, wg, rsnd, rrcv, psnd, pout,
           lsem, sems, sx, rx, sw, rw, ss, rs):
    d = lax.axis_index("dp")
    z = lax.axis_index("tensor")
    core = lax.rem(d, 2)
    chip = lax.div(d, 2)
    x, y = lax.rem(chip, 4), lax.div(chip, 4)

    def copy(src, dst, ss, rs, dev):
        return pltpu.make_async_remote_copy(src_ref=src, dst_ref=dst, send_sem=ss, recv_sem=rs, device_id=dev,
                                            device_id_type=pl.DeviceIdType.MESH)

    def each(n, f):
        def body(i, carry):
            f(i)
            return carry
        lax.fori_loop(1, n, body, 0)

    twin = (d + 1 - 2 * core, z)
    opened = []

    class Flow:
        def __init__(self, n, src, dst, to, number):
            self.n, self.src, self.dst, self.to = n, src, dst, to
            self.sems = (sems.at[0, number], sems.at[1, number])
            self.got = False

        def one(self, i):
            dev, source, place = self.to(i)
            copy(self.src.at[source], self.dst.at[place], *self.sems, dev).start()

        def start(self):
            each(self.n, self.one)
            opened.append(self)

        def all(self):
            ref = self.src.at[pl.ds(0, self.n - 1)]
            return copy(ref, ref, *self.sems, twin)

        def recv(self):
            self.all().wait_recv()
            self.got = True

        def sent(self):
            self.all().wait_send()
            opened.remove(self)

    class Single:
        def __init__(self, c):
            self.c, self.got = c, False

        def start(self):
            self.c.start()
            opened.append(self)

        def recv(self):
            self.c.wait_recv()
            self.got = True

        def sent(self):
            self.c.wait_send()
            opened.remove(self)

    def finish():
        for flow in list(opened):
            if not flow.got:
                flow.recv()
            flow.sent()

    def over_z(i):
        to = lax.rem(z + i, NZ)
        return (d, to), to, z

    def over_z_same(i):
        return (d, lax.rem(z + i, NZ)), z, z

    def over_dp(i):
        to = lax.rem(d + i, ND)
        return (to, z), to, d

    def over_chips(i):
        to = lax.rem(chip + i, NC)
        return (2 * to + core, z), to, chip

    def over_chips_same(i):
        return (2 * lax.rem(chip + i, NC) + core, z), chip, chip

    slices = Flow(NZ, snd, own, over_z, 0)
    deliver = Flow(ND, pk, prcv, over_dp, 1)
    reduce = Flow(NZ, zs, zr, over_z, 2)
    share = Flow(NZ, red, red, over_z_same, 3)
    give_back = Flow(ND, er, back, over_dp, 4)
    results = Flow(NZ, rsnd, rrcv, over_z, 5)
    plane = Flow(NC, psnd, pout, over_chips, 6)
    scatter = Flow(NC, half, hot_in, over_chips, 7)
    gather = Flow(NC, hot.at[core], hot.at[core], over_chips_same, 8)
    swap = Single(copy(mine.at[1 - core], twin_in, sems.at[0, 9], sems.at[1, 9], twin))
    swap_hot = Single(copy(hot.at[core], hot.at[core], sems.at[0, 10], sems.at[1, 10], twin))

    first = x * (1 - core) + y * core
    second = y * (1 - core) + x * core

    def spot(a, b):
        return lax.rem(a, 4) * (1 + 3 * core) + lax.rem(b, 4) * (4 - 3 * core)

    def pdev(a, b):
        return (2 * spot(a, b) + core, z)

    near1 = (pdev(first + 1, second), pdev(first + 3, second))
    near2 = (pdev(first, second + 1), pdev(first, second + 3))
    kept = {}

    def keep(key, make):
        if key not in kept:
            kept[key] = Single(make())
        return kept[key]

    def line(way, hop):
        def make():
            if hop == 0:
                return copy(att, buf.at[chip], sx.at[0, way, 0], rx.at[0, way, 0], near1[way])
            ref = buf.at[spot(first + (3 if way == 0 else 1), second), pl.ds(16 * way, 16)]
            return copy(ref, ref, sx.at[0, way, 1], rx.at[0, way, 1], near1[way])
        return keep(("line", way, hop), make)

    def sheet(way, hop, j):
        def make():
            col = first + (0, 3, 1, 2)[j]
            if hop == 0:
                dst = buf.at[spot(col, second)]
                src = att if j == 0 else dst
            else:
                dst = buf.at[spot(col, second + (3 if way == 0 else 1)), pl.ds(16 * way, 16)]
                src = dst
            return copy(src, dst, sx.at[1 + hop, way, j], rx.at[1 + hop, way, j], near2[way])
        return keep(("sheet", way, hop, j), make)

    right, left = (d, lax.rem(z + 1, NZ)), (d, lax.rem(z + NZ - 1, NZ))

    def ring(way, step, part):
        def make():
            block = lax.rem(z + (NZ - step if way == 0 else step), NZ)
            lanes = pl.ds(0, CUT) if part == 0 else pl.ds(CUT, LANES - CUT)
            ref = wg.at[core, block, :, lanes]
            return copy(ref, ref, sw.at[way, step, part], rw.at[way, step, part], right if way == 0 else left)
        return keep(("ring", way, step, part), make)

    def moves(step):
        return [(way, part) for part in range(2) for way in range(2) if step < 7 or way == part]

    def tell(o):
        def make():
            ref = wg.at[core, lax.rem(z + o, NZ)]
            return copy(ref, ref, ss.at[o], rs.at[o], twin)
        return keep(("tell", o), make)

    def ring_step(step):
        for way, part in moves(step):
            if step > 0:
                ring(way, step - 1, part).recv()
            ring(way, step, part).start()
        if step == 0:
            tell(0).start()
        elif step < 7:
            tell(step).start()
            tell(NZ - step).start()

    def ring_end():
        for way, part in moves(6):
            if not ring(way, 6, part).got:
                ring(way, 6, part).recv()
        tell(7).start()
        tell(9).start()
        for way, part in moves(7):
            ring(way, 7, part).recv()
        tell(8).start()

    def line_on():
        for way in range(2):
            line(way, 0).recv()
            line(way, 1).start()
            for to in range(2):
                sheet(to, 0, 1 + way).start()

    def line_end():
        for way in range(2):
            line(way, 1).recv()
        for to in range(2):
            sheet(to, 0, 3).start()

    def sheet_on(j):
        for way in range(2):
            sheet(way, 0, j).recv()
            sheet(way, 1, j).start()

    barrier = pltpu.get_barrier_semaphore()
    each(NZ, lambda i: pl.semaphore_signal(barrier, inc=1, device_id=over_z(i)[0], device_id_type=pl.DeviceIdType.MESH))
    each(ND, lambda i: pl.semaphore_signal(barrier, inc=1, device_id=over_dp(i)[0], device_id_type=pl.DeviceIdType.MESH))
    lanes_half = pl.ds(pl.multiple_of(core * HALF, HALF), HALF)
    loads = [pltpu.make_async_copy(h, v, lsem.at[i]) for i, (h, v) in enumerate((
        (w_h.at[pl.ds(pl.multiple_of(16 * chip, 16), 16), lanes_half], wg.at[core, z, :, pl.ds(0, HALF)]),
        (w_h.at[pl.ds(MAIN, REST), lanes_half], wr), (a_h, av), (b_h, bv), (res_h, res)))]
    for load in loads:
        load.start()
    for t in range(NZ):
        snd[t] = att[:, COLS * t:COLS * t + COLS]
    own[z] = snd[z]
    matrix, ids, is_busy = routing(ten[...], idx[...], d)
    pick[...] = matrix
    for load in loads:
        load.wait()
    n, c = iota((16, REST), 0), iota((16, REST), 1)
    low = dot(onehot((c == 4 * chip + n) & (n < 4)), wr[...])
    wg[core, z, :, HALF:] = jnp.concatenate([low[:4, QUART * q:QUART * q + QUART] for q in range(4)], axis=0).astype(BF)
    mark = is_busy.astype(BF)
    for i in range(2 * NC):
        e, r = i // 4, 16 * (i % 4)
        mine[i // NC, i % NC, :16] = av[e, r:r + 16] * mark
        mine[i // NC, i % NC, 16:] = bv[e, r:r + 16] * mark
    pl.semaphore_wait(barrier, NZ + ND - 2)

    slices.start()
    for way in range(2):
        line(way, 0).start()
    for way in range(2):
        sheet(way, 0, 0).start()
    swap.start()
    buf[chip] = att[...]
    swap.recv()
    half[...] = mine[core] + twin_in[...]
    hot_in[chip] = half[chip]
    scatter.start()
    line_on()
    sheet_on(0)
    line_end()
    scatter.recv()
    hot[core, chip] = jnp.sum(hot_in[...].astype(F32), axis=0).astype(BF)
    gather.start()
    ring_step(0)
    sheet_on(1)
    ring_step(1)
    sheet_on(2)
    ring_step(2)
    slices.recv()
    ext = jnp.concatenate([own[...].reshape(TOK, COLS), ids], axis=1)
    pk[...] = dot(pick[...], ext).astype(BF).reshape(ND, SLOT, COLS + 64)
    prcv[d] = pk[d]
    deliver.start()
    ring_step(3)
    sheet_on(3)
    ring_step(4)
    gather.recv()
    swap_hot.start()
    deliver.recv()
    swap_hot.recv()
    got = prcv[...].reshape(TOK, COLS + 64)
    rows, ident = got[:, :COLS], got[:, COLS:COLS + 1].astype(F32)
    group = (iota((1, HOT), 1) // RANK + 1).astype(F32)
    hot_all = hot[...].reshape(ND, 32, COLS)
    hot_a, hot_b = hot_all[:, :16].reshape(HOT, COLS), hot_all[:, 16:].reshape(HOT, COLS)
    total = jnp.where(ident == group, dot_nt(rows, av[...].reshape(HOT, COLS)), 0.0)
    total += jnp.where(ident == group + ADP, dot_nt(rows, hot_a), 0.0)
    total = total[:, :128] + total[:, 128:256] + total[:, 256:384] + total[:, 384:]
    part = (total[:, :RANK] + total[:, RANK:]).astype(BF)
    for t in range(NZ):
        zs[t] = jnp.concatenate([part[32 * t:32 * t + 16], part[32 * t + 16:32 * t + 32]], axis=1)
    zr[z] = zs[z]
    reduce.start()
    ring_step(5)
    for j in range(4):
        for way in range(2):
            sheet(way, 1, j).recv()
    quarter = iota((MAIN, 1), 0) % 16 // 4
    zero = jnp.zeros((), BF)

    def project(offsets):
        for o in offsets:
            tell(o).recv()
        blocks = [lax.rem(z + o, NZ) for o in offsets]
        count = 16 * len(blocks)
        main = jnp.zeros((count, TOK), F32)
        rest = jnp.zeros((count, TOK), F32)
        for h in range(2):
            for q in range(4):
                at = QUART * q
                toks = buf[:, :, HALF * h + at:HALF * h + at + QUART].reshape(TOK, QUART)
                tail = jnp.concatenate([wg[h, b, :, HALF:] for b in blocks], axis=0)
                left = jnp.concatenate([wg[h, b, :, at:at + QUART] for b in blocks]
                                       + [jnp.where(quarter[:count] == q, tail, zero)], axis=0)
                both = dot_nt(left, toks)
                main += both[:count]
                rest += both[count:]
        for n, b in enumerate(blocks):
            s = rest[16 * n:16 * n + 8] + rest[16 * n + 8:16 * n + 16]
            s = s[:4] + s[4:]
            tail = jnp.concatenate([s[:, 128 * j:128 * j + 128] for j in range(4)], axis=0)
            rsnd[b] = jnp.concatenate([main[16 * n:16 * n + 16], tail], axis=1).astype(BF)
        for o in offsets:
            if o:
                results.one(o)

    project((1,15,2,14,3,13,4,12,0,))
    ring_step(6)
    project((5,11,))
    reduce.recv()
    red[z] = jnp.sum(zr[...].astype(F32), axis=0).astype(BF)
    share.start()
    ring_step(7)
    project((6,10,))
    ring_end()
    project((7,9,8,))
    share.recv()
    for t in range(NZ):
        sh[32 * t:32 * t + 16] = red[t, :, :RANK]
        sh[32 * t + 16:32 * t + 32] = red[t, :, RANK:]
    wide = jnp.concatenate([sh[...]] * ADP, axis=1)
    expand = dot(jnp.where(ident == group, wide, zero), bv[...].reshape(HOT, COLS))
    expand += dot(jnp.where(ident == group + ADP, wide, zero), hot_b)
    er[...] = expand.astype(BF).reshape(ND, SLOT, COLS)
    back[d] = er[d]
    give_back.start()
    opened.append(results)
    rrcv[z] = rsnd[z]
    results.recv()
    pieces = []
    for g in range(4):
        four = jnp.concatenate([rrcv[4 * g + i] for i in range(4)], axis=1)
        for j in range(5):
            pieces.append(jnp.concatenate(
                [four[:, 640 * i + 128 * j:640 * i + 128 * j + 128] for i in range(4)], axis=1))
    stacked = jnp.concatenate(pieces, axis=0)
    lane_in, lane_out = iota((TOK, TOK), 0), iota((TOK, TOK), 1)
    moved = (lane_in // 32 % 4) * 128 + lane_in // 128 * 32 + lane_in % 32
    turned = dot(stacked, onehot(moved == lane_out))
    for j in range(NC):
        t, k = j // 4, 128 * (j % 4)
        for g in range(4):
            psnd[j, 16 * g:16 * g + 16] = turned[80 * g + 16 * t:80 * g + 16 * t + 16, k:k + 128].astype(BF)
        psnd[j, 64:] = jnp.concatenate(
            [turned[80 * g + 64 + 4 * t:80 * g + 68 + 4 * t, k:k + 128] for g in range(4)], axis=0).astype(BF)
    pout[chip] = psnd[chip]
    plane.start()
    give_back.recv()
    extra = dot_t(back[...].reshape(TOK, COLS), pick[...])
    plane.recv()
    upright = [jnp.concatenate([pout[p, 16 * g:16 * g + 16] for g in range(4)], axis=1).astype(F32) for p in range(NC)]
    for p in range(NC):
        low = pout[p, 64:].astype(F32)
        upright.append(jnp.concatenate([low[4 * g:4 * g + 4] for g in range(4)], axis=1))
    base = jnp.concatenate(upright, axis=0)
    out[...] = (res[...].astype(F32) + base + 0.5 * extra).astype(BF)
    finish()


def local(attention, residual, output_weight, adapter_down_weight, adapter_up_weight, tenant, adapter_slot_index):
    vmem = pl.BlockSpec(memory_space=pltpu.VMEM)
    hbm = pl.BlockSpec(memory_space=pl.ANY)
    dma = pltpu.SemaphoreType.DMA

    def held(*shape, dtype=BF):
        return pltpu.VMEM(shape, dtype)

    return pl.pallas_call(
        kernel,
        out_shape=jax.ShapeDtypeStruct((COLS, TOK), BF),
        in_specs=[vmem, hbm, hbm, hbm, hbm, vmem, vmem],
        out_specs=vmem,
        scratch_shapes=[
            held(REST, HALF), held(COLS, TOK), held(ADP, RANK, COLS), held(ADP, RANK, COLS),
            held(2, NC, 32, COLS), held(NC, 32, COLS), held(NC, 32, COLS), held(NC, 32, COLS), held(2, NC, 32, COLS),
            held(NZ, OWN, COLS), held(NZ, OWN, COLS), held(TOK, TOK),
            held(ND, SLOT, COLS + 64), held(ND, SLOT, COLS + 64),
            held(NZ, 16, 128), held(NZ, 16, 128), held(NZ, 16, 128), held(TOK, RANK),
            held(ND, SLOT, COLS), held(ND, SLOT, COLS),
            held(NC, OWN, WIDTH), held(2, NZ, 16, LANES), held(NZ, 16, 640), held(NZ, 16, 640),
            held(NC, 80, 128), held(NC, 80, 128),
            dma((5,)), dma((2, 11)), dma((3, 2, 4)), dma((3, 2, 4)), dma((2, 8, 2)), dma((2, 8, 2)), dma((NZ,)), dma((NZ,)),
        ],
        compiler_params=pltpu.CompilerParams(collective_id=0, has_side_effects=True, vmem_limit_bytes=56 * 2**20),
    )(attention, residual.T, output_weight.T, adapter_down_weight.transpose(0, 2, 1), adapter_up_weight,
      tenant.reshape(1, REQ), adapter_slot_index.reshape(1, 2 * REQ)).T


def solution(mesh):
    in_specs = (
        P(("dp", "tensor"), None),
        P("dp", "tensor"),
        P(None, "tensor"),
        P("dp", "tensor", None),
        P("dp", None, "tensor"),
        P("dp"),
        P(),
    )
    return jax.shard_map(local, mesh=mesh, in_specs=in_specs, out_specs=P("dp", "tensor"), check_vma=False)
```

```python
import jax
import jax.numpy as jnp
from jax import lax
from jax.experimental import pallas as pl
from jax.experimental.pallas import tpu as pltpu
from jax.sharding import PartitionSpec as P

BF = jnp.bfloat16
F32 = jnp.float32
ND, NZ = 32, 16
DRAFT, REQ, TOK = 4, 128, 512
WIDTH, COLS, RANK, ADP = 5120, 320, 64, 8
OWN = TOK // NZ
SLOT = TOK // ND
HOT = ADP * RANK
HALF = WIDTH // 2
NC = 16
MAIN, REST = 256, 64
QUART = HALF // 4
LANES = HALF + QUART
CUT = 1664


def iota(shape, axis):
    return lax.broadcasted_iota(jnp.int32, shape, axis)


def dot(a, b):
    return jnp.dot(a, b, preferred_element_type=F32)


def dot_t(a, b):
    return lax.dot_general(a, b, (((0,), (0,)), ((), ())), preferred_element_type=F32)


def onehot(mask):
    return jnp.where(mask, 1.0, 0.0).astype(BF)


def dot_nt(a, b):
    return lax.dot_general(a, b, (((1,), (1,)), ((), ())), preferred_element_type=F32)


def routing(tenant, index, me):
    hit = onehot(iota((2 * REQ, REQ), 0) == tenant)
    slot = dot(jnp.broadcast_to(index, (8, 2 * REQ)).astype(F32).astype(BF), hit)[0:1]
    owner = jnp.floor(slot * (1.0 / ADP))
    adapter = slot - ADP * owner
    owner_id = iota((ND, REQ), 0).astype(F32)
    own_hit = jnp.where(owner_id == owner, 1.0, 0.0)
    before = onehot(iota((REQ, REQ), 0) < iota((REQ, REQ), 1))
    place = jnp.sum(own_hit * dot(own_hit.astype(BF), before), axis=0, keepdims=True)
    count = jnp.sum(own_hit, axis=1, keepdims=True)
    busy = jnp.where(count > 4.5, 1.0, 0.0)
    busy_req = jnp.sum(own_hit * busy, axis=0, keepdims=True)
    count = jnp.broadcast_to(count * (1.0 - busy), (ND, REQ)).astype(BF)
    is_busy = jnp.sum(busy * jnp.where(owner_id[:, 0:1] == me.astype(F32), 1.0, 0.0), axis=0, keepdims=True)
    slot_row = iota((REQ, REQ), 0)
    filled = dot(onehot(iota((REQ, ND), 0) // 4 == iota((REQ, ND), 1)), count)
    free = jnp.where((slot_row % 4).astype(F32) >= filled, 1.0, 0.0)
    rank = dot(onehot(iota((REQ, REQ), 1) < slot_row), free.astype(BF))
    to_free = free * jnp.where(rank == place, 1.0, 0.0) * busy_req
    to_own = jnp.where(slot_row.astype(F32) == 4.0 * owner + place, 1.0, 0.0) * (1.0 - busy_req)
    by_request = (to_free + to_own).astype(BF)
    spread = onehot(iota((REQ, TOK), 0) == iota((REQ, TOK), 1) // DRAFT)
    gather = onehot(iota((TOK, REQ), 0) // DRAFT == iota((TOK, REQ), 1))
    rows = dot(dot(gather, by_request).astype(BF), spread)
    same = iota((TOK, TOK), 0) % DRAFT == iota((TOK, TOK), 1) % DRAFT
    matrix = jnp.where(same, rows, 0.0).astype(BF)
    ident = adapter + 1.0 + ADP * busy_req
    eye = iota((REQ, REQ), 0) == iota((REQ, REQ), 1)
    column = jnp.sum(jnp.where(eye, ident, 0.0), axis=1, keepdims=True)
    ids = dot(gather, jnp.broadcast_to(column, (REQ, 64)).astype(BF)).astype(BF)
    return matrix, ids, is_busy


def kernel(att, res_h, w_h, a_h, b_h, ten, idx, out, wr, res, av, bv, mine, twin_in, half, hot_in, hot,
           snd, own, pick, pk, prcv, zs, zr, red, sh, er, back, buf, wg, rsnd, rrcv, psnd, pout,
           lsem, sems, sx, rx, sw, rw, ss, rs):
    d = lax.axis_index("dp")
    z = lax.axis_index("tensor")
    core = lax.rem(d, 2)
    chip = lax.div(d, 2)
    x, y = lax.rem(chip, 4), lax.div(chip, 4)

    def copy(src, dst, ss, rs, dev):
        return pltpu.make_async_remote_copy(src_ref=src, dst_ref=dst, send_sem=ss, recv_sem=rs, device_id=dev,
                                            device_id_type=pl.DeviceIdType.MESH)

    def each(n, f):
        def body(i, carry):
            f(i)
            return carry
        lax.fori_loop(1, n, body, 0)

    twin = (d + 1 - 2 * core, z)
    opened = []

    class Flow:
        def __init__(self, n, src, dst, to, number):
            self.n, self.src, self.dst, self.to = n, src, dst, to
            self.sems = (sems.at[0, number], sems.at[1, number])
            self.got = False

        def one(self, i):
            dev, source, place = self.to(i)
            copy(self.src.at[source], self.dst.at[place], *self.sems, dev).start()

        def start(self):
            each(self.n, self.one)
            opened.append(self)

        def all(self):
            ref = self.src.at[pl.ds(0, self.n - 1)]
            return copy(ref, ref, *self.sems, twin)

        def recv(self):
            self.all().wait_recv()
            self.got = True

        def sent(self):
            self.all().wait_send()
            opened.remove(self)

    class Single:
        def __init__(self, c):
            self.c, self.got = c, False

        def start(self):
            self.c.start()
            opened.append(self)

        def recv(self):
            self.c.wait_recv()
            self.got = True

        def sent(self):
            self.c.wait_send()
            opened.remove(self)

    def finish():
        for flow in list(opened):
            if not flow.got:
                flow.recv()
            flow.sent()

    def over_z(i):
        to = lax.rem(z + i, NZ)
        return (d, to), to, z

    def over_z_same(i):
        return (d, lax.rem(z + i, NZ)), z, z

    def over_dp(i):
        to = lax.rem(d + i, ND)
        return (to, z), to, d

    def over_chips(i):
        to = lax.rem(chip + i, NC)
        return (2 * to + core, z), to, chip

    def over_chips_same(i):
        return (2 * lax.rem(chip + i, NC) + core, z), chip, chip

    slices = Flow(NZ, snd, own, over_z, 0)
    deliver = Flow(ND, pk, prcv, over_dp, 1)
    reduce = Flow(NZ, zs, zr, over_z, 2)
    share = Flow(NZ, red, red, over_z_same, 3)
    give_back = Flow(ND, er, back, over_dp, 4)
    results = Flow(NZ, rsnd, rrcv, over_z, 5)
    plane = Flow(NC, psnd, pout, over_chips, 6)
    scatter = Flow(NC, half, hot_in, over_chips, 7)
    gather = Flow(NC, hot.at[core], hot.at[core], over_chips_same, 8)
    swap = Single(copy(mine.at[1 - core], twin_in, sems.at[0, 9], sems.at[1, 9], twin))
    swap_hot = Single(copy(hot.at[core], hot.at[core], sems.at[0, 10], sems.at[1, 10], twin))

    first = x * (1 - core) + y * core
    second = y * (1 - core) + x * core

    def spot(a, b):
        return lax.rem(a, 4) * (1 + 3 * core) + lax.rem(b, 4) * (4 - 3 * core)

    def pdev(a, b):
        return (2 * spot(a, b) + core, z)

    near1 = (pdev(first + 1, second), pdev(first + 3, second))
    near2 = (pdev(first, second + 1), pdev(first, second + 3))
    kept = {}

    def keep(key, make):
        if key not in kept:
            kept[key] = Single(make())
        return kept[key]

    def line(way, hop):
        def make():
            if hop == 0:
                return copy(att, buf.at[chip], sx.at[0, way, 0], rx.at[0, way, 0], near1[way])
            ref = buf.at[spot(first + (3 if way == 0 else 1), second), pl.ds(16 * way, 16)]
            return copy(ref, ref, sx.at[0, way, 1], rx.at[0, way, 1], near1[way])
        return keep(("line", way, hop), make)

    def sheet(way, hop, j):
        def make():
            col = first + (0, 3, 1, 2)[j]
            if hop == 0:
                dst = buf.at[spot(col, second)]
                src = att if j == 0 else dst
            else:
                dst = buf.at[spot(col, second + (3 if way == 0 else 1)), pl.ds(16 * way, 16)]
                src = dst
            return copy(src, dst, sx.at[1 + hop, way, j], rx.at[1 + hop, way, j], near2[way])
        return keep(("sheet", way, hop, j), make)

    right, left = (d, lax.rem(z + 1, NZ)), (d, lax.rem(z + NZ - 1, NZ))

    def ring(way, step, part):
        def make():
            block = lax.rem(z + (NZ - step if way == 0 else step), NZ)
            lanes = pl.ds(0, CUT) if part == 0 else pl.ds(CUT, LANES - CUT)
            ref = wg.at[core, block, :, lanes]
            return copy(ref, ref, sw.at[way, step, part], rw.at[way, step, part], right if way == 0 else left)
        return keep(("ring", way, step, part), make)

    def moves(step):
        return [(way, part) for part in range(2) for way in range(2) if step < 7 or way == part]

    def tell(o):
        def make():
            ref = wg.at[core, lax.rem(z + o, NZ)]
            return copy(ref, ref, ss.at[o], rs.at[o], twin)
        return keep(("tell", o), make)

    def ring_step(step):
        for way, part in moves(step):
            if step > 0:
                ring(way, step - 1, part).recv()
            ring(way, step, part).start()
        if step == 0:
            tell(0).start()
        elif step < 7:
            tell(step).start()
            tell(NZ - step).start()

    def ring_end():
        for way, part in moves(6):
            if not ring(way, 6, part).got:
                ring(way, 6, part).recv()
        tell(7).start()
        tell(9).start()
        for way, part in moves(7):
            ring(way, 7, part).recv()
        tell(8).start()

    def line_on():
        for way in range(2):
            line(way, 0).recv()
            line(way, 1).start()
            for to in range(2):
                sheet(to, 0, 1 + way).start()

    def line_end():
        for way in range(2):
            line(way, 1).recv()
        for to in range(2):
            sheet(to, 0, 3).start()

    def sheet_on(j):
        for way in range(2):
            sheet(way, 0, j).recv()
            sheet(way, 1, j).start()

    barrier = pltpu.get_barrier_semaphore()
    each(NZ, lambda i: pl.semaphore_signal(barrier, inc=1, device_id=over_z(i)[0], device_id_type=pl.DeviceIdType.MESH))
    each(ND, lambda i: pl.semaphore_signal(barrier, inc=1, device_id=over_dp(i)[0], device_id_type=pl.DeviceIdType.MESH))
    lanes_half = pl.ds(pl.multiple_of(core * HALF, HALF), HALF)
    loads = [pltpu.make_async_copy(h, v, lsem.at[i]) for i, (h, v) in enumerate((
        (w_h.at[pl.ds(pl.multiple_of(16 * chip, 16), 16), lanes_half], wg.at[core, z, :, pl.ds(0, HALF)]),
        (w_h.at[pl.ds(MAIN, REST), lanes_half], wr), (a_h, av), (b_h, bv), (res_h, res)))]
    for load in loads:
        load.start()
    for t in range(NZ):
        snd[t] = att[:, COLS * t:COLS * t + COLS]
    own[z] = snd[z]
    matrix, ids, is_busy = routing(ten[...], idx[...], d)
    pick[...] = matrix
    for load in loads:
        load.wait()
    n, c = iota((16, REST), 0), iota((16, REST), 1)
    low = dot(onehot((c == 4 * chip + n) & (n < 4)), wr[...])
    wg[core, z, :, HALF:] = jnp.concatenate([low[:4, QUART * q:QUART * q + QUART] for q in range(4)], axis=0).astype(BF)
    mark = is_busy.astype(BF)
    for i in range(2 * NC):
        e, r = i // 4, 16 * (i % 4)
        mine[i // NC, i % NC, :16] = av[e, r:r + 16] * mark
        mine[i // NC, i % NC, 16:] = bv[e, r:r + 16] * mark
    pl.semaphore_wait(barrier, NZ + ND - 2)

    slices.start()
    for way in range(2):
        line(way, 0).start()
    for way in range(2):
        sheet(way, 0, 0).start()
    swap.start()
    buf[chip] = att[...]
    swap.recv()
    half[...] = mine[core] + twin_in[...]
    hot_in[chip] = half[chip]
    scatter.start()
    ring_step(0)
    line_on()
    sheet_on(0)
    line_end()
    ring_step(1)
    slices.recv()
    ext = jnp.concatenate([own[...].reshape(TOK, COLS), ids], axis=1)
    pk[...] = dot(pick[...], ext).astype(BF).reshape(ND, SLOT, COLS + 64)
    prcv[d] = pk[d]
    deliver.start()
    scatter.recv()
    hot[core, chip] = jnp.sum(hot_in[...].astype(F32), axis=0).astype(BF)
    gather.start()
    sheet_on(1)
    ring_step(2)
    sheet_on(2)
    ring_step(3)
    ring_step(4)
    sheet_on(3)
    ring_step(5)
    gather.recv()
    swap_hot.start()
    ring_step(6)
    deliver.recv()
    swap_hot.recv()
    got = prcv[...].reshape(TOK, COLS + 64)
    rows, ident = got[:, :COLS], got[:, COLS:COLS + 1].astype(F32)
    group = (iota((1, HOT), 1) // RANK + 1).astype(F32)
    hot_all = hot[...].reshape(ND, 32, COLS)
    hot_a, hot_b = hot_all[:, :16].reshape(HOT, COLS), hot_all[:, 16:].reshape(HOT, COLS)
    total = jnp.where(ident == group, dot_nt(rows, av[...].reshape(HOT, COLS)), 0.0)
    total += jnp.where(ident == group + ADP, dot_nt(rows, hot_a), 0.0)
    total = total[:, :128] + total[:, 128:256] + total[:, 256:384] + total[:, 384:]
    part = (total[:, :RANK] + total[:, RANK:]).astype(BF)
    for t in range(NZ):
        zs[t] = jnp.concatenate([part[32 * t:32 * t + 16], part[32 * t + 16:32 * t + 32]], axis=1)
    zr[z] = zs[z]
    reduce.start()
    ring_step(7)
    for j in range(4):
        for way in range(2):
            sheet(way, 1, j).recv()
    quarter = iota((MAIN, 1), 0) % 16 // 4
    zero = jnp.zeros((), BF)

    def project(offsets):
        for o in offsets:
            tell(o).recv()
        blocks = [lax.rem(z + o, NZ) for o in offsets]
        count = 16 * len(blocks)
        main = jnp.zeros((count, TOK), F32)
        rest = jnp.zeros((count, TOK), F32)
        for h in range(2):
            for q in range(4):
                at = QUART * q
                toks = buf[:, :, HALF * h + at:HALF * h + at + QUART].reshape(TOK, QUART)
                tail = jnp.concatenate([wg[h, b, :, HALF:] for b in blocks], axis=0)
                left = jnp.concatenate([wg[h, b, :, at:at + QUART] for b in blocks]
                                       + [jnp.where(quarter[:count] == q, tail, zero)], axis=0)
                both = dot_nt(left, toks)
                main += both[:count]
                rest += both[count:]
        for n, b in enumerate(blocks):
            s = rest[16 * n:16 * n + 8] + rest[16 * n + 8:16 * n + 16]
            s = s[:4] + s[4:]
            tail = jnp.concatenate([s[:, 128 * j:128 * j + 128] for j in range(4)], axis=0)
            rsnd[b] = jnp.concatenate([main[16 * n:16 * n + 16], tail], axis=1).astype(BF)
        for o in offsets:
            if o:
                results.one(o)

    project((1,15,2,14,3,13,4,12,0,))
    ring_end()
    reduce.recv()
    red[z] = jnp.sum(zr[...].astype(F32), axis=0).astype(BF)
    share.start()
    project((5,11,6,10,7,9,8,))
    share.recv()
    for t in range(NZ):
        sh[32 * t:32 * t + 16] = red[t, :, :RANK]
        sh[32 * t + 16:32 * t + 32] = red[t, :, RANK:]
    wide = jnp.concatenate([sh[...]] * ADP, axis=1)
    expand = dot(jnp.where(ident == group, wide, zero), bv[...].reshape(HOT, COLS))
    expand += dot(jnp.where(ident == group + ADP, wide, zero), hot_b)
    er[...] = expand.astype(BF).reshape(ND, SLOT, COLS)
    back[d] = er[d]
    give_back.start()
    opened.append(results)
    rrcv[z] = rsnd[z]
    results.recv()
    pieces = []
    for g in range(4):
        four = jnp.concatenate([rrcv[4 * g + i] for i in range(4)], axis=1)
        for j in range(5):
            pieces.append(jnp.concatenate(
                [four[:, 640 * i + 128 * j:640 * i + 128 * j + 128] for i in range(4)], axis=1))
    stacked = jnp.concatenate(pieces, axis=0)
    lane_in, lane_out = iota((TOK, TOK), 0), iota((TOK, TOK), 1)
    moved = (lane_in // 32 % 4) * 128 + lane_in // 128 * 32 + lane_in % 32
    turned = dot(stacked, onehot(moved == lane_out))
    for j in range(NC):
        t, k = j // 4, 128 * (j % 4)
        for g in range(4):
            psnd[j, 16 * g:16 * g + 16] = turned[80 * g + 16 * t:80 * g + 16 * t + 16, k:k + 128].astype(BF)
        psnd[j, 64:] = jnp.concatenate(
            [turned[80 * g + 64 + 4 * t:80 * g + 68 + 4 * t, k:k + 128] for g in range(4)], axis=0).astype(BF)
    pout[chip] = psnd[chip]
    plane.start()
    give_back.recv()
    extra = dot_t(back[...].reshape(TOK, COLS), pick[...])
    plane.recv()
    upright = [jnp.concatenate([pout[p, 16 * g:16 * g + 16] for g in range(4)], axis=1).astype(F32) for p in range(NC)]
    for p in range(NC):
        low = pout[p, 64:].astype(F32)
        upright.append(jnp.concatenate([low[4 * g:4 * g + 4] for g in range(4)], axis=1))
    base = jnp.concatenate(upright, axis=0)
    out[...] = (res[...].astype(F32) + base + 0.5 * extra).astype(BF)
    finish()


def local(attention, residual, output_weight, adapter_down_weight, adapter_up_weight, tenant, adapter_slot_index):
    vmem = pl.BlockSpec(memory_space=pltpu.VMEM)
    hbm = pl.BlockSpec(memory_space=pl.ANY)
    dma = pltpu.SemaphoreType.DMA

    def held(*shape, dtype=BF):
        return pltpu.VMEM(shape, dtype)

    return pl.pallas_call(
        kernel,
        out_shape=jax.ShapeDtypeStruct((COLS, TOK), BF),
        in_specs=[vmem, hbm, hbm, hbm, hbm, vmem, vmem],
        out_specs=vmem,
        scratch_shapes=[
            held(REST, HALF), held(COLS, TOK), held(ADP, RANK, COLS), held(ADP, RANK, COLS),
            held(2, NC, 32, COLS), held(NC, 32, COLS), held(NC, 32, COLS), held(NC, 32, COLS), held(2, NC, 32, COLS),
            held(NZ, OWN, COLS), held(NZ, OWN, COLS), held(TOK, TOK),
            held(ND, SLOT, COLS + 64), held(ND, SLOT, COLS + 64),
            held(NZ, 16, 128), held(NZ, 16, 128), held(NZ, 16, 128), held(TOK, RANK),
            held(ND, SLOT, COLS), held(ND, SLOT, COLS),
            held(NC, OWN, WIDTH), held(2, NZ, 16, LANES), held(NZ, 16, 640), held(NZ, 16, 640),
            held(NC, 80, 128), held(NC, 80, 128),
            dma((5,)), dma((2, 11)), dma((3, 2, 4)), dma((3, 2, 4)), dma((2, 8, 2)), dma((2, 8, 2)), dma((NZ,)), dma((NZ,)),
        ],
        compiler_params=pltpu.CompilerParams(collective_id=0, has_side_effects=True, vmem_limit_bytes=56 * 2**20),
    )(attention, residual.T, output_weight.T, adapter_down_weight.transpose(0, 2, 1), adapter_up_weight,
      tenant.reshape(1, REQ), adapter_slot_index.reshape(1, 2 * REQ)).T


def solution(mesh):
    in_specs = (
        P(("dp", "tensor"), None),
        P("dp", "tensor"),
        P(None, "tensor"),
        P("dp", "tensor", None),
        P("dp", None, "tensor"),
        P("dp"),
        P(),
    )
    return jax.shard_map(local, mesh=mesh, in_specs=in_specs, out_specs=P("dp", "tensor"), check_vma=False)
```
